512 devices in a mesh: group: 64 (over z_hi, y, x), tensor: 8 (over z_lo, core).
Axes of the slice: x: 4, y: 8, z: 8 (z_hi: 2, z_lo: 4; z = z_hi * 4 + z_lo), core: 2. Of those that a mesh axis runs over, the one named last changes fastest.
Arguments:
- queries: bfloat16 [1024, 2, 8192], P('group', None, 'tensor'), may hold values from -42 to 42
- new_kv: bfloat16 [1024, 2, 2, 1024], P('group', None, None, 'tensor'), may hold values from -42 to 42
- own_kv: bfloat16 [1024, 256, 2, 1024], P('group', None, None, 'tensor'), may hold values from -42 to 42
- prefix_kv: bfloat16 [64, 4096, 2, 8, 128], P('group', 'tensor'), may hold values from -15 to 15
- owner: int32 [64], replicated, may hold values from 0 to 63, as said below
- parent: int32 [1024], P('group'), may hold values from 0 to 63, as said below
- own_len: int32 [1024], P('group'), may hold values from 2 to 256, as said below
Outputs:
- attended: bfloat16 [1024, 2, 8192], P('group', None, 'tensor')
The draws below stay inside these ranges and needn't reach their ends.
Inputs may be any that keep to these rules, and one draw needn't show every extreme that they name: `owner`: each group holds exactly one node's prefix. The owner of a row's parent lies 1 to 6 groups before the row's group, counted cyclically; in every draw some row lies exactly 6 groups after it. `own_len`: some row has all 256 slots live.
All inputs are finite; a program needn't handle non-finite values.
Results may differ from the reference program's by a relative error of at most 0.015.
Values may be sent and summed in bfloat16 or wider, within the bound.
No kernel may reach another device: no remote copies, remote signals or barrier semaphores. Data moves between devices by JAX's collectives and lax.ppermute only.
A program may use at most 64 MiB of HBM per device.

```python
import jax
import jax.numpy as jnp
from jax import lax

QH = 64
KVH = 8
HD = 128
PLEN = 4096
OWN = 256
ROWS_DEV = 16
DRAFT = 2
MAXFAN = 6
NODES = 64
ROWS = 1024


def tree_layout(key):
    layout_key = jax.random.fold_in(key, 7)
    perm_key, fan_key = jax.random.split(layout_key)
    owner = jax.random.permutation(perm_key, NODES).astype(jnp.int32)
    fanout = jax.random.randint(fan_key, (NODES,), 2, MAXFAN + 1).astype(jnp.int32)
    fanout = fanout.at[0].set(MAXFAN)
    return (owner, fanout)


def shared_latent(key):
    latent_key = jax.random.fold_in(key, 3)
    first_key, second_key, third_key = jax.random.split(latent_key, 3)
    latent = jnp.clip(jax.random.normal(first_key, (ROWS, DRAFT, KVH, HD), jnp.float32), -6.0, 6.0)
    noise = jnp.clip(jax.random.normal(second_key, (ROWS, DRAFT, KVH, HD), jnp.float32), -6.0, 6.0)
    spread = jax.random.uniform(third_key, (ROWS,), jnp.float32)
    return (latent, noise, spread)


def draw_owner(key, part):
    owner, fanout = tree_layout(key)
    return owner


def draw_parent(key, part):
    owner, fanout = tree_layout(key)
    key = jax.random.fold_in(key, 13)
    holder = jnp.zeros((NODES,), jnp.int32).at[owner].set(jnp.arange(NODES, dtype=jnp.int32))
    row_ids = jnp.arange(ROWS, dtype=jnp.int32)
    groups = row_ids // ROWS_DEV
    reaches = jnp.arange(1, MAXFAN + 1, dtype=jnp.int32)
    sources = (groups[:, None] - reaches[None, :]) % NODES
    candidates = holder[sources]
    usable = fanout[candidates] >= reaches[None, :]
    scores = jax.random.randint(key, (ROWS, MAXFAN), 0, 1 << 20) * (2 * MAXFAN) + reaches[None, :]
    scores = jnp.where(usable, scores, -1)
    forced_row = ROWS_DEV * ((owner[0] + MAXFAN) % NODES)
    forced = (row_ids[:, None] == forced_row) & (reaches[None, :] == MAXFAN)
    scores = jnp.where(forced, 1 << 30, scores)
    picked = jnp.argmax(scores, axis=1)
    return jnp.take_along_axis(candidates, picked[:, None], axis=1)[:, 0].astype(jnp.int32)


def draw_own_len(key, part):
    key = jax.random.fold_in(key, 17)
    first_key, second_key = jax.random.split(key)
    lengths = jax.random.randint(first_key, (ROWS,), 2, OWN + 1).astype(jnp.int32)
    longest = jax.random.randint(second_key, (), 0, ROWS)
    return jnp.where(jnp.arange(ROWS) == longest, OWN, lengths).astype(jnp.int32)


def draw_queries(key, part):
    latent, noise, spread = shared_latent(key)
    key = jax.random.fold_in(key, 21)
    strength = jnp.ones_like(spread)
    per_kv = QH // KVH
    aligned = 0.85 * strength[:, None, None, None] * latent
    extra = jnp.clip(jax.random.normal(key, (ROWS, DRAFT, KVH, per_kv, HD), jnp.float32), -6.0, 6.0)
    result = aligned[:, :, :, None, :] + 0.53 * extra
    return result.reshape(ROWS, DRAFT, QH * HD).astype(jnp.bfloat16)


def draw_new_kv(key, part):
    latent, noise, spread = shared_latent(key)
    key = jax.random.fold_in(key, 25)
    strength = jnp.ones_like(spread)
    keys_part = 0.75 * strength[:, None, None, None] * latent + 0.66 * noise
    keys_part = keys_part.reshape(ROWS, DRAFT, KVH * HD)
    values_part = jnp.clip(jax.random.normal(key, (ROWS, DRAFT, KVH * HD), jnp.float32), -6.0, 6.0)
    return jnp.stack([keys_part, values_part], axis=2).astype(jnp.bfloat16)


def draw_own_kv(key, part):
    key = jax.random.fold_in(key, 31)
    first_key, second_key = jax.random.split(key)
    keys_part = 2.5 * jnp.clip(jax.random.normal(first_key, (ROWS, OWN, KVH * HD), jnp.float32), -6.0, 6.0)
    values_part = jnp.clip(jax.random.normal(second_key, (ROWS, OWN, KVH * HD), jnp.float32), -6.0, 6.0)
    return jnp.stack([keys_part, values_part], axis=2).astype(jnp.bfloat16)


def block_scale(own_key, extent, shards, least, high):
    factor_of, own = 1.0, jax.random.fold_in(own_key, 6)
    for dim, shards_of in shards:
        heights = jnp.exp(jax.random.uniform(jax.random.fold_in(own, dim), (shards_of,), jnp.float32, least / len(shards), high / len(shards)))
        factor_of = factor_of * jnp.repeat(heights, extent[dim] // shards_of).reshape([-1 if axis == dim else 1 for axis in range(len(extent))])
    return factor_of


def centred(rng, shape, width, most, shards=(), kind=jnp.bfloat16):
    entries = width * jax.random.normal(rng, shape, jnp.float32)
    if shards:
        entries = entries * block_scale(rng, shape, shards, -0.22, 0.18)
    return jnp.clip(entries, -most, most).astype(kind)


def setup_inputs(seed: int = 0) -> dict:
    key_list = jax.random.split(jax.random.key(seed), 8)
    queries = draw_queries(jax.random.fold_in(key_list[7], 71), 0)
    new_kv = draw_new_kv(jax.random.fold_in(key_list[7], 71), 0)
    own_kv = draw_own_kv(jax.random.fold_in(key_list[7], 71), 0)
    prefix_kv = centred(key_list[3], (NODES, PLEN, 2, KVH, HD), 2.5, 15.0, ((0, 64), (1, 8)))
    owner = draw_owner(jax.random.fold_in(key_list[7], 71), 0)
    parent = draw_parent(jax.random.fold_in(key_list[7], 71), 0)
    own_len = draw_own_len(jax.random.fold_in(key_list[7], 71), 0)
    return {"queries": queries, "new_kv": new_kv, "own_kv": own_kv, "prefix_kv": prefix_kv, "owner": owner, "parent": parent, "own_len": own_len}


def attend_rows(queries, new_kv, own_kv, own_len, prefix):
    row_count = queries.shape[0]
    per_kv = QH // KVH
    scaling = HD ** -0.5
    query_f = queries.astype(jnp.float32).reshape(row_count, DRAFT, KVH, per_kv, HD)
    prefix_keys = prefix[:, :, 0].astype(jnp.float32)
    prefix_values = prefix[:, :, 1].astype(jnp.float32)
    own_cache = own_kv.astype(jnp.float32).reshape(row_count, OWN, 2, KVH, HD)
    new_cache = new_kv.astype(jnp.float32).reshape(row_count, DRAFT, 2, KVH, HD)
    s_prefix = jnp.einsum("rtkjd,rpkd->rtkjp", query_f, prefix_keys) * scaling
    s_own = jnp.einsum("rtkjd,rpkd->rtkjp", query_f, own_cache[:, :, 0]) * scaling
    s_new = jnp.einsum("rtkjd,rukd->rtkju", query_f, new_cache[:, :, 0]) * scaling
    live_mask = jnp.arange(OWN)[None, :] < own_len[:, None]
    s_own = jnp.where(live_mask[:, None, None, None, :], s_own, -jnp.inf)
    causal = jnp.arange(DRAFT)[None, :] <= jnp.arange(DRAFT)[:, None]
    s_new = jnp.where(causal[None, :, None, None, :], s_new, -jnp.inf)
    maxima = jnp.maximum(jnp.maximum(s_prefix.max(-1), s_own.max(-1)), s_new.max(-1))
    w_prefix = jnp.exp(s_prefix - maxima[..., None])
    w_own = jnp.exp(s_own - maxima[..., None])
    w_new = jnp.exp(s_new - maxima[..., None])
    totals = w_prefix.sum(-1) + w_own.sum(-1) + w_new.sum(-1)

    def rounded(weights):
        return lax.optimization_barrier(weights.astype(jnp.bfloat16)).astype(jnp.float32)

    summed = jnp.einsum("rtkjp,rpkd->rtkjd", rounded(w_prefix), prefix_values)
    summed = summed + jnp.einsum("rtkjp,rpkd->rtkjd", rounded(w_own), own_cache[:, :, 1])
    summed = summed + jnp.einsum("rtkju,rukd->rtkjd", rounded(w_new), new_cache[:, :, 1])
    result = summed / totals[..., None]
    return result.astype(jnp.bfloat16).reshape(row_count, DRAFT, QH * HD)


def reference(queries, new_kv, own_kv, prefix_kv, owner, parent, own_len):
    slot = owner[parent]

    def one_group(group_index):
        first_row = (group_index * ROWS_DEV).astype(jnp.int32)

        def take_rows(array):
            return lax.dynamic_slice_in_dim(array, first_row, ROWS_DEV, 0)

        prefix = prefix_kv[take_rows(slot)]
        return attend_rows(take_rows(queries), take_rows(new_kv), take_rows(own_kv), take_rows(own_len), prefix)

    result = lax.map(one_group, jnp.arange(NODES, dtype=jnp.int32))
    return result.reshape(ROWS, DRAFT, QH * HD)
```

```python
import functools

import jax
import jax.numpy as jnp
from jax import lax
from jax.experimental import pallas as pl
from jax.experimental.pallas import tpu as pltpu
from jax.sharding import PartitionSpec as P

WINDOW = 8
DRAFT = 2
BLOCK_ROWS = 16
FENCE_FLOPS = 20_000_000_000
VMEM_BYTES = 48 * 1024 * 1024


def nt_dot(left, right):
    return lax.dot_general(left, right, (((1,), (1,)), ((), ())), preferred_element_type=jnp.float32)


def local_kernel(len_ref, q_ref, kv_ref, out_ref, lse_ref):
    rows, vectors, head_dim = q_ref.shape
    slots = kv_ref.shape[2]
    cached = slots - 16
    scaling = head_dim ** (-0.5)
    place = lax.broadcasted_iota(jnp.int32, (vectors, slots), 1)
    token = lax.broadcasted_iota(jnp.int32, (vectors, slots), 0) // (vectors // DRAFT)
    fresh = (place >= cached) & (place - cached <= token)
    for row in range(rows):
        scores = nt_dot(q_ref[row], kv_ref[row, 0]) * scaling
        live = (place < jnp.minimum(len_ref[row], cached)) | fresh
        scores = jnp.where(live, scores, -jnp.inf)
        maxima = scores.max(-1, keepdims=True)
        weights = jnp.exp(scores - maxima)
        totals = weights.sum(-1, keepdims=True)
        summed = jnp.dot(
            weights.astype(jnp.bfloat16), kv_ref[row, 1], preferred_element_type=jnp.float32
        )
        out_ref[row] = summed / totals
        lse_ref[row] = jnp.broadcast_to(maxima + jnp.log(totals), (vectors, head_dim))


def local_attention(queries, own_kv, new_kv, own_len):
    rows, vectors, head_dim = queries.shape
    cache = jnp.concatenate([own_kv, new_kv], axis=1)
    cache = jnp.pad(cache, ((0, 0), (0, 16 - DRAFT), (0, 0), (0, 0)))
    cache = cache.transpose(0, 2, 1, 3)
    shape = jax.ShapeDtypeStruct((rows, vectors, head_dim), jnp.float32)
    vmem = pl.BlockSpec(memory_space=pltpu.VMEM)
    return pl.pallas_call(
        local_kernel,
        out_shape=(shape, shape),
        in_specs=[pl.BlockSpec(memory_space=pltpu.SMEM), vmem, vmem],
        out_specs=(vmem, vmem),
        compiler_params=pltpu.CompilerParams(vmem_limit_bytes=VMEM_BYTES),
        cost_estimate=pl.CostEstimate(flops=300_000_000, bytes_accessed=2_500_000, transcendentals=70_000),
        name="local_attention",
    )(own_len, queries, cache)


def prefix_kernel(live_ref, q_ref, *rest):
    *kv_refs, out_ref, packed, scores, stats, index = rest
    cells, heads, tiles, vectors, head_dim = q_ref.shape
    rows = tiles - 1
    chunk = kv_refs[0].shape[2]
    width = BLOCK_ROWS * vectors
    scaling = head_dim ** (-0.5)

    out_ref[...] = jnp.zeros_like(out_ref)
    stats[...] = jnp.zeros_like(stats)
    packed[...] = jnp.zeros_like(packed)

    def pack(slot, count):
        cell, row = slot // rows, slot % rows
        for head in range(heads):
            packed[head, count] = q_ref[cell, head, row]
        index[count] = slot
        return count + live_ref[slot]

    count = lax.fori_loop(0, cells * rows, pack, jnp.int32(0), unroll=4)

    lane = lax.broadcasted_iota(jnp.int32, (vectors, head_dim), 1)
    vector = lax.broadcasted_iota(jnp.int32, (vectors, head_dim), 0)
    on_lane = (lane % vectors == vector) & (lane < 3 * vectors)
    piece = lane // vectors

    def block(step, carry):
        first = step * BLOCK_ROWS
        for head in range(heads):
            q = packed[head, pl.ds(first, BLOCK_ROWS)].reshape(width, head_dim)
            maxima = None
            for part, kv in enumerate(kv_refs):
                product = nt_dot(q, kv[head, 0]) * scaling
                scores[part] = product
                top = product.max(-1, keepdims=True)
                maxima = top if maxima is None else jnp.maximum(maxima, top)
            totals = jnp.zeros((width, 1), jnp.float32)
            summed = jnp.zeros((width, head_dim), jnp.float32)
            for part, kv in enumerate(kv_refs):
                weights = jnp.exp(scores[part] - maxima)
                totals = totals + weights.sum(-1, keepdims=True)
                summed = summed + jnp.dot(
                    weights.astype(jnp.bfloat16), kv[head, 1], preferred_element_type=jnp.float32
                )
            attended = (summed / totals).astype(jnp.bfloat16)
            level = jnp.broadcast_to(maxima + jnp.log(totals), (width, head_dim))
            high = level.astype(jnp.bfloat16).astype(jnp.float32)
            middle = (level - high).astype(jnp.bfloat16).astype(jnp.float32)
            low = level - high - middle
            for row in range(BLOCK_ROWS):
                span = slice(row * vectors, (row + 1) * vectors)
                pieces = jnp.where(piece == 0, high[span], jnp.where(piece == 1, middle[span], low[span]))
                line = jnp.where(on_lane, pieces, 0.0).sum(0, keepdims=True)

                @pl.when(first + row < count)
                def _(row=row, span=span, line=line):
                    slot = index[first + row]
                    out_ref[slot // rows, head, slot % rows] = attended[span]
                    stats[head, pl.ds(slot, 1), :] = line

        return carry

    lax.fori_loop(0, (count + BLOCK_ROWS - 1) // BLOCK_ROWS, block, 0)
    for cell in range(cells):
        for head in range(heads):
            out_ref[cell, head, rows] = stats[head, cell * rows : (cell + 1) * rows, :].astype(jnp.bfloat16)


def prefix_attention(live, arrived, blocks):
    cells, heads, tiles, vectors, head_dim = arrived.shape
    slots = cells * (tiles - 1)
    chunk = blocks[0].shape[2]
    vmem = pl.BlockSpec(memory_space=pltpu.VMEM)
    return pl.pallas_call(
        prefix_kernel,
        out_shape=jax.ShapeDtypeStruct(arrived.shape, jnp.bfloat16),
        in_specs=[pl.BlockSpec(memory_space=pltpu.SMEM)] + [vmem] * (1 + len(blocks)),
        out_specs=vmem,
        scratch_shapes=[
            pltpu.VMEM((heads, slots + BLOCK_ROWS, vectors, head_dim), jnp.bfloat16),
            pltpu.VMEM((len(blocks), BLOCK_ROWS * vectors, chunk), jnp.float32),
            pltpu.VMEM((heads, slots, head_dim), jnp.float32),
            pltpu.SMEM((slots + 1,), jnp.int32),
        ],
        compiler_params=pltpu.CompilerParams(vmem_limit_bytes=VMEM_BYTES),
        cost_estimate=pl.CostEstimate(flops=1_000_000_000, bytes_accessed=4_000_000, transcendentals=2_000_000),
        name="prefix_attention",
    )(live, arrived, *blocks)


def merge_kernel(*refs):
    *part_refs, local_ref, local_lse_ref, out_ref = refs
    rows, vectors, head_dim = local_ref.shape
    lane = lax.broadcasted_iota(jnp.int32, (vectors, head_dim), 1)
    vector = lax.broadcasted_iota(jnp.int32, (vectors, head_dim), 0)
    on_lane = (lane % vectors == vector) & (lane < 3 * vectors)
    pairs = [part_refs[k : k + 2] for k in range(0, len(part_refs), 2)]
    levels = [one[rows].astype(jnp.float32) + other[rows].astype(jnp.float32) for one, other in pairs]
    for row in range(rows):
        terms = [(local_ref[row], local_lse_ref[row])]
        for (one, other), level in zip(pairs, levels):
            line = jnp.broadcast_to(level[row : row + 1], (vectors, head_dim))
            lse = jnp.where(on_lane, line, 0.0).sum(-1, keepdims=True)
            attended = one[row].astype(jnp.float32) + other[row].astype(jnp.float32)
            terms.append((attended, jnp.broadcast_to(lse, (vectors, head_dim))))
        maxima = functools.reduce(jnp.maximum, [lse for _, lse in terms])
        scales = [jnp.exp(lse - maxima) for _, lse in terms]
        summed = sum(scale * term for scale, (term, _) in zip(scales, terms))
        out_ref[row] = (summed / sum(scales)).astype(jnp.bfloat16)


def merge_parts(parts, local, local_lse):
    vmem = pl.BlockSpec(memory_space=pltpu.VMEM)
    return pl.pallas_call(
        merge_kernel,
        out_shape=jax.ShapeDtypeStruct(local.shape, jnp.bfloat16),
        in_specs=[vmem] * (len(parts) + 2),
        out_specs=vmem,
        compiler_params=pltpu.CompilerParams(vmem_limit_bytes=VMEM_BYTES),
        name="merge_parts",
    )(*parts, local, local_lse)


def split_kernel(lane_ref, prefix_ref, *rest):
    *out_refs, by_head = rest
    positions, sides, heads, head_dim = prefix_ref.shape
    quad = len(out_refs)
    for side in range(sides):
        by_head[side] = jnp.swapaxes(prefix_ref[:, side], 0, 1)
    for step, out_ref in enumerate(out_refs):
        first = lane_ref[0] ^ step
        for half in range(heads // quad):
            for side in range(sides):
                out_ref[half, side] = by_head[side, first + half * quad]


def split_prefix(lane, prefix):
    positions, sides, heads, head_dim = prefix.shape
    quad = heads // 2
    shape = jax.ShapeDtypeStruct((2, sides, positions, head_dim), prefix.dtype)
    vmem = pl.BlockSpec(memory_space=pltpu.VMEM)
    return pl.pallas_call(
        split_kernel,
        out_shape=[shape] * quad,
        in_specs=[pl.BlockSpec(memory_space=pltpu.SMEM), vmem],
        out_specs=[vmem] * quad,
        scratch_shapes=[pltpu.VMEM((sides, heads, positions, head_dim), prefix.dtype)],
        compiler_params=pltpu.CompilerParams(vmem_limit_bytes=VMEM_BYTES),
        cost_estimate=pl.CostEstimate(flops=0, bytes_accessed=4 * 1024 * 1024, transcendentals=0),
        name="split_prefix",
    )(lane.reshape(1), prefix)


def fence_kernel(*refs):
    del refs


def fence(arrays):
    place = pl.BlockSpec(memory_space=pl.ANY)
    return pl.pallas_call(
        fence_kernel,
        out_shape=[jax.ShapeDtypeStruct(x.shape, x.dtype) for x in arrays],
        in_specs=[place] * len(arrays),
        out_specs=[place] * len(arrays),
        input_output_aliases={k: k for k in range(len(arrays))},
        cost_estimate=pl.CostEstimate(flops=FENCE_FLOPS, bytes_accessed=0, transcendentals=0),
        name="fence",
    )(*arrays)


def moved(x, by, flip=0):
    groups, lanes = lax.axis_size("group"), lax.axis_size("tensor")
    pairs = [
        (g * lanes + t, (g + by) % groups * lanes + (t ^ flip)) for g in range(groups) for t in range(lanes)
    ]
    return lax.ppermute(x, ("group", "tensor"), pairs)


def windowed(x):
    groups = lax.axis_size("group")
    windows = [list(range(first, first + WINDOW)) for first in range(0, groups, WINDOW)]
    return lax.all_to_all(x, "group", 0, 0, axis_index_groups=windows, tiled=True)


def on_device(queries, new_kv, own_kv, prefix_kv, owner, parent, own_len):
    rows, draft, width = queries.shape
    head_dim = prefix_kv.shape[4]
    per_kv = width // head_dim
    vectors = draft * per_kv
    me = lax.axis_index("group")
    lane = lax.axis_index("tensor")
    place = me % WINDOW
    cells = jnp.arange(WINDOW)

    distance = (me - owner[parent]) % lax.axis_size("group")
    tag = jnp.broadcast_to(distance.astype(jnp.bfloat16)[None, :, None], (1, rows, head_dim))
    q = queries.reshape(rows, vectors, head_dim)
    sent = jnp.concatenate([q, tag.reshape(1, vectors, head_dim)])
    quad = prefix_kv.shape[3] // 2
    partner = moved(sent, 0, quad)
    blocks = split_prefix(lane % quad, prefix_kv[0])
    *blocks, partner = lax.optimization_barrier([*blocks, partner])
    blocks = blocks[:1] + list(fence([moved(blocks[step], 0, step) for step in range(1, quad)]))
    upper = lane >= quad

    def both(own, other):
        return jnp.where(upper, jnp.stack([other, own]), jnp.stack([own, other]))

    here = both(sent, partner)
    after = moved(here, -WINDOW)
    mine = (cells < place)[:, None, None, None, None]
    arrived = windowed(jnp.where(mine, here, after))
    tags = arrived[:, 0, rows, :, 0].astype(jnp.int32)
    live = (tags > 0) & (tags == ((cells - place) % WINDOW)[:, None])
    local, local_lse = local_attention(q, own_kv, new_kv, own_len)
    arrived, local, local_lse = lax.optimization_barrier((arrived, local, local_lse))
    partial = prefix_attention(live.reshape(-1).astype(jnp.int32), arrived, blocks)

    returned = windowed(partial)
    here = jnp.where(mine, returned, 0).sum(0)
    after = jnp.where(mine, 0, returned).sum(0)
    here_own, here_other = jnp.where(upper, here[1], here[0]), jnp.where(upper, here[0], here[1])
    after_own, after_other = jnp.where(upper, after[1], after[0]), jnp.where(upper, after[0], after[1])
    parts = [here_own, moved(after_own, WINDOW), moved(here_other, 0, quad), moved(after_other, WINDOW, quad)]
    return merge_parts(parts, local, local_lse).reshape(rows, draft, width)


def solution(mesh):
    placed = (
        P("group", None, "tensor"),
        P("group", None, None, "tensor"),
        P("group", None, None, "tensor"),
        P("group", "tensor", None, None, None),
        P(),
        P("group"),
        P("group"),
    )
    return jax.shard_map(
        on_device, mesh=mesh, in_specs=placed, out_specs=P("group", None, "tensor"), check_vma=False
    )
```

```python
import functools
import math

import jax
import jax.numpy as jnp
from jax import lax
from jax.experimental import pallas as pl
from jax.experimental.pallas import tpu as pltpu
from jax.sharding import PartitionSpec as P

WINDOW = 8
DRAFT = 2
BLOCK_ROWS = 16
FLIPS = ((0,), (1,), (2, 3), (4,), (5,), (6,), (7,))
STAGE_FLOPS = 10_000_000_000
LOCAL_FLOPS = 20_000_000_000
VMEM_BYTES = 16 * 1024 * 1024


def nt_dot(left, right):
    return lax.dot_general(left, right, (((1,), (1,)), ((), ())), preferred_element_type=jnp.float32)


def local_kernel(len_ref, q_ref, kv_ref, out_ref, lse_ref, scores):
    rows, vectors, head_dim = q_ref.shape
    slots = kv_ref.shape[2]
    cached = slots - 16
    scaling = head_dim ** (-0.5)
    place = lax.broadcasted_iota(jnp.int32, (vectors, slots), 1)
    token = lax.broadcasted_iota(jnp.int32, (vectors, slots), 0) // (vectors // DRAFT)
    fresh = (place >= cached) & (place - cached <= token)
    for row in range(rows):
        live = (place < jnp.minimum(len_ref[row], cached)) | fresh
        scores[row] = jnp.where(live, nt_dot(q_ref[row], kv_ref[row, 0]) * scaling, -jnp.inf)
    maxima = scores[...].max(-1, keepdims=True)
    weights = jnp.exp(scores[...] - maxima)
    totals = weights.sum(-1, keepdims=True)
    lse_ref[...] = jnp.broadcast_to(maxima + jnp.log(totals), lse_ref.shape)
    inverse = 1.0 / totals
    rounded = weights.astype(jnp.bfloat16)
    for row in range(rows):
        summed = jnp.dot(rounded[row], kv_ref[row, 1], preferred_element_type=jnp.float32)
        out_ref[row] = summed * inverse[row]


def local_attention(queries, own_kv, new_kv, own_len):
    rows, vectors, head_dim = queries.shape
    cache = jnp.concatenate([own_kv, new_kv], axis=1)
    cache = jnp.pad(cache, ((0, 0), (0, 16 - DRAFT), (0, 0), (0, 0)))
    cache = cache.transpose(0, 2, 1, 3)
    shape = jax.ShapeDtypeStruct((rows, vectors, head_dim), jnp.float32)
    vmem = pl.BlockSpec(memory_space=pltpu.VMEM)
    return pl.pallas_call(
        local_kernel,
        out_shape=(shape, shape),
        in_specs=[pl.BlockSpec(memory_space=pltpu.SMEM), vmem, vmem],
        out_specs=(vmem, vmem),
        scratch_shapes=[pltpu.VMEM((rows, vectors, cache.shape[2]), jnp.float32)],
        compiler_params=pltpu.CompilerParams(vmem_limit_bytes=VMEM_BYTES),
        cost_estimate=pl.CostEstimate(flops=LOCAL_FLOPS, bytes_accessed=2_500_000, transcendentals=70_000),
        name="local_attention",
    )(own_len, queries, cache)


def attend_block(q, kv_refs, scores):
    width, head_dim = q.shape
    scaling = head_dim ** (-0.5)
    maxima = None
    for part, kv in enumerate(kv_refs):
        product = nt_dot(q, kv[0])
        scores[part] = product
        top = product.max(-1, keepdims=True)
        maxima = top if maxima is None else jnp.maximum(maxima, top)
    base2 = scaling * math.log2(math.e)
    shift = maxima * base2
    totals = jnp.zeros((width, 1), jnp.float32)
    summed = jnp.zeros((width, head_dim), jnp.float32)
    for part, kv in enumerate(kv_refs):
        weights = jnp.exp2(scores[part] * base2 - shift)
        totals = totals + weights.sum(-1, keepdims=True)
        summed = summed + jnp.dot(weights.astype(jnp.bfloat16), kv[1], preferred_element_type=jnp.float32)
    level = jnp.broadcast_to(maxima * scaling + jnp.log(totals), (width, head_dim))
    return summed / totals, level


def pack_kernel(live_ref, q_ref, packed, index):
    cells, tiles, vectors, head_dim = q_ref.shape
    rows = tiles - 1
    packed[...] = jnp.zeros_like(packed)
    count = jnp.int32(0)
    for slot in range(cells * rows):
        packed[count] = q_ref[slot // rows, slot % rows]
        index[count] = slot
        count = count + live_ref[slot]
    index[cells * rows + 1] = count


def pack_queries(live, arrived):
    cells, tiles, vectors, head_dim = arrived.shape
    slots = cells * (tiles - 1)
    vmem, smem = pl.BlockSpec(memory_space=pltpu.VMEM), pl.BlockSpec(memory_space=pltpu.SMEM)
    return pl.pallas_call(
        pack_kernel,
        out_shape=(
            jax.ShapeDtypeStruct((slots + BLOCK_ROWS, vectors, head_dim), jnp.bfloat16),
            jax.ShapeDtypeStruct((slots + 2,), jnp.int32),
        ),
        in_specs=[smem, vmem],
        out_specs=(vmem, smem),
        compiler_params=pltpu.CompilerParams(vmem_limit_bytes=VMEM_BYTES),
        name="pack_queries",
    )(live, arrived)


def merged(first, second):
    top = jnp.maximum(first[1], second[1])
    first_scale, second_scale = jnp.exp(first[1] - top), jnp.exp(second[1] - top)
    totals = first_scale + second_scale
    return (first[0] * first_scale + second[0] * second_scale) / totals, top + jnp.log(totals)


def stage_kernel(parts, halves, index, packed, *rest):
    state, kv_refs, outs, scores = rest[: 2 * parts], rest[2 * parts : -3], rest[-3:-1], rest[-1]
    kv_refs = [kv if half is None else kv.at[half] for kv, half in zip(kv_refs, halves)]
    width, head_dim = outs[0].shape[1:]
    count = index[index.shape[0] - 1]

    def block(step, carry):
        q = packed[pl.ds(step * BLOCK_ROWS, BLOCK_ROWS)].reshape(width, head_dim)
        total = attend_block(q, kv_refs, scores)
        if parts:
            total = merged(total, (state[0][step], state[1][step]))
        outs[0][step], outs[1][step] = total
        return carry

    lax.fori_loop(0, (count + BLOCK_ROWS - 1) // BLOCK_ROWS, block, 0)


def attend_stage(index, packed, state, blocks, halves=(None, None)):
    slots, vectors, head_dim = packed.shape[0] - BLOCK_ROWS, *packed.shape[1:]
    chunk = blocks[0].shape[-2]
    width = BLOCK_ROWS * vectors
    vmem, smem = pl.BlockSpec(memory_space=pltpu.VMEM), pl.BlockSpec(memory_space=pltpu.SMEM)
    shape = jax.ShapeDtypeStruct((slots // BLOCK_ROWS, width, head_dim), jnp.float32)
    return pl.pallas_call(
        functools.partial(stage_kernel, len(state) // 2, halves),
        out_shape=(shape, shape),
        in_specs=[smem] + [vmem] * (1 + len(state) + len(blocks)),
        out_specs=(vmem, vmem),
        scratch_shapes=[pltpu.VMEM((len(blocks), width, chunk), jnp.float32)],
        compiler_params=pltpu.CompilerParams(vmem_limit_bytes=VMEM_BYTES),
        cost_estimate=pl.CostEstimate(flops=STAGE_FLOPS, bytes_accessed=2_000_000, transcendentals=0),
        name="attend_stage",
    )(index, packed, *state, *blocks)


def late_kernel(index, packed, attended_ref, level_ref, *rest):
    *kv_refs, out_ref, scores, stats = rest
    cells, tiles, vectors, head_dim = out_ref.shape
    rows = tiles - 1
    width = BLOCK_ROWS * vectors
    out_ref[...] = jnp.zeros_like(out_ref)
    stats[...] = jnp.zeros_like(stats)
    count = index[cells * rows + 1]

    lane = lax.broadcasted_iota(jnp.int32, (vectors, head_dim), 1)
    vector = lax.broadcasted_iota(jnp.int32, (vectors, head_dim), 0)
    on_lane = (lane % vectors == vector) & (lane < 3 * vectors)
    piece = lane // vectors

    def block(step, carry):
        first = step * BLOCK_ROWS
        q = packed[pl.ds(first, BLOCK_ROWS)].reshape(width, head_dim)
        late = attend_block(q, kv_refs, scores)
        attended, level = merged(late, (attended_ref[step], level_ref[step]))
        attended = attended.astype(jnp.bfloat16)
        high = level.astype(jnp.bfloat16).astype(jnp.float32)
        middle = (level - high).astype(jnp.bfloat16).astype(jnp.float32)
        low = level - high - middle
        for row in range(BLOCK_ROWS):
            span = slice(row * vectors, (row + 1) * vectors)
            pieces = jnp.where(piece == 0, high[span], jnp.where(piece == 1, middle[span], low[span]))
            line = jnp.where(on_lane, pieces, 0.0).sum(0, keepdims=True)

            @pl.when(first + row < count)
            def _(row=row, span=span, line=line):
                slot = index[first + row]
                out_ref[slot // rows, slot % rows] = attended[span]
                stats[pl.ds(slot, 1), :] = line

        return carry

    lax.fori_loop(0, (count + BLOCK_ROWS - 1) // BLOCK_ROWS, block, 0)
    for cell in range(cells):
        out_ref[cell, rows] = stats[cell * rows : (cell + 1) * rows, :].astype(jnp.bfloat16)


def attend_late(shape, index, packed, state, blocks):
    cells, tiles, vectors, head_dim = shape
    slots = cells * (tiles - 1)
    chunk = blocks[0].shape[-2]
    width = BLOCK_ROWS * vectors
    vmem, smem = pl.BlockSpec(memory_space=pltpu.VMEM), pl.BlockSpec(memory_space=pltpu.SMEM)
    return pl.pallas_call(
        late_kernel,
        out_shape=jax.ShapeDtypeStruct(shape, jnp.bfloat16),
        in_specs=[smem] + [vmem] * (3 + len(blocks)),
        out_specs=vmem,
        scratch_shapes=[
            pltpu.VMEM((len(blocks), width, chunk), jnp.float32),
            pltpu.VMEM((slots, head_dim), jnp.float32),
        ],
        compiler_params=pltpu.CompilerParams(vmem_limit_bytes=VMEM_BYTES),
        cost_estimate=pl.CostEstimate(flops=STAGE_FLOPS, bytes_accessed=4_000_000, transcendentals=0),
        name="attend_late",
    )(index, packed, *state, *blocks)


def merge_kernel(*refs):
    *part_refs, local_ref, local_lse_ref, out_ref = refs
    rows, vectors, head_dim = local_ref.shape
    lane = lax.broadcasted_iota(jnp.int32, (vectors, head_dim), 1)
    vector = lax.broadcasted_iota(jnp.int32, (vectors, head_dim), 0)
    on_lane = (lane % vectors == vector) & (lane < 3 * vectors)
    pairs = [part_refs[k : k + 2] for k in range(0, len(part_refs), 2)]
    levels = [one[rows].astype(jnp.float32) + other[rows].astype(jnp.float32) for one, other in pairs]
    for row in range(rows):
        terms = [(local_ref[row], local_lse_ref[row])]
        for (one, other), level in zip(pairs, levels):
            line = jnp.broadcast_to(level[row : row + 1], (vectors, head_dim))
            lse = jnp.where(on_lane, line, 0.0).sum(-1, keepdims=True)
            attended = one[row].astype(jnp.float32) + other[row].astype(jnp.float32)
            terms.append((attended, jnp.broadcast_to(lse, (vectors, head_dim))))
        maxima = functools.reduce(jnp.maximum, [lse for _, lse in terms])
        scales = [jnp.exp(lse - maxima) for _, lse in terms]
        summed = sum(scale * term for scale, (term, _) in zip(scales, terms))
        out_ref[row] = (summed / sum(scales)).astype(jnp.bfloat16)


def merge_parts(parts, local, local_lse):
    vmem = pl.BlockSpec(memory_space=pltpu.VMEM)
    return pl.pallas_call(
        merge_kernel,
        out_shape=jax.ShapeDtypeStruct(local.shape, jnp.bfloat16),
        in_specs=[vmem] * (len(parts) + 2),
        out_specs=vmem,
        compiler_params=pltpu.CompilerParams(vmem_limit_bytes=VMEM_BYTES),
        name="merge_parts",
    )(*parts, local, local_lse)


def split_kernel(lane_ref, prefix_ref, *rest):
    *out_refs, by_head = rest
    sides = prefix_ref.shape[1]
    for side in range(sides):
        by_head[side] = jnp.swapaxes(prefix_ref[:, side], 0, 1)
    for out_ref, flips in zip(out_refs, FLIPS):
        for half, flip in enumerate(flips):
            for side in range(sides):
                target = out_ref if len(flips) == 1 else out_ref.at[half]
                target[side] = by_head[side, lane_ref[0] ^ flip]


def split_prefix(lane, prefix):
    positions, sides, heads, head_dim = prefix.shape
    shape = (sides, positions, head_dim)
    vmem = pl.BlockSpec(memory_space=pltpu.VMEM)
    return pl.pallas_call(
        split_kernel,
        out_shape=[
            jax.ShapeDtypeStruct(shape if len(flips) == 1 else (len(flips), *shape), prefix.dtype)
            for flips in FLIPS
        ],
        in_specs=[pl.BlockSpec(memory_space=pltpu.SMEM), vmem],
        out_specs=[vmem] * len(FLIPS),
        scratch_shapes=[pltpu.VMEM((sides, heads, positions, head_dim), prefix.dtype)],
        compiler_params=pltpu.CompilerParams(vmem_limit_bytes=VMEM_BYTES),
        cost_estimate=pl.CostEstimate(flops=0, bytes_accessed=4 * 1024 * 1024, transcendentals=0),
        name="split_prefix",
    )(lane.reshape(1), prefix)


def moved(x, by, flip=0):
    groups, lanes = lax.axis_size("group"), lax.axis_size("tensor")
    pairs = [
        (g * lanes + t, (g + by) % groups * lanes + (t ^ flip)) for g in range(groups) for t in range(lanes)
    ]
    return lax.ppermute(x, ("group", "tensor"), pairs)


def windowed(x):
    groups = lax.axis_size("group")
    windows = [list(range(first, first + WINDOW)) for first in range(0, groups, WINDOW)]
    return lax.all_to_all(x, "group", 0, 0, axis_index_groups=windows, tiled=True)


def on_device(queries, new_kv, own_kv, prefix_kv, owner, parent, own_len):
    rows, draft, width = queries.shape
    heads, head_dim = prefix_kv.shape[3:]
    per_kv = width // head_dim
    vectors = draft * per_kv
    me = lax.axis_index("group")
    place = me % WINDOW
    cells = jnp.arange(WINDOW)

    q = queries.reshape(rows, vectors, head_dim)
    distance = (me - owner[parent]) % lax.axis_size("group")
    tag = jnp.broadcast_to(distance.astype(jnp.bfloat16)[None, :, None], (1, rows, head_dim))
    sent = jnp.concatenate([q, tag.reshape(1, vectors, head_dim)])
    own, beside, near, *far = split_prefix(lax.axis_index("tensor"), prefix_kv[0])
    far = [moved(block, 0, 4 + step) for step, block in enumerate(far)]
    beside, sent = lax.optimization_barrier((moved(beside, 0, 1), sent))
    near, after = moved(near, 0, 2), moved(sent, -WINDOW)

    mine = (cells < place)[:, None, None, None]
    cell = jnp.where(mine, sent, after)
    arrived = windowed(cell)
    tags = arrived[:, rows, :, 0].astype(jnp.int32)
    live = (tags > 0) & (tags == ((cells - place) % WINDOW)[:, None])
    own_kv, new_kv, cell = lax.optimization_barrier((own_kv, new_kv, cell))
    late_q, near = lax.optimization_barrier((q, near))
    local, local_lse = local_attention(late_q, own_kv, new_kv, own_len)
    arrived, local, local_lse = lax.optimization_barrier((arrived, local, local_lse))
    packed, index = pack_queries(live.reshape(-1).astype(jnp.int32), arrived)
    near_beside = moved(near, 0, 1)
    state = attend_stage(index, packed, (), [own, beside, near, near_beside], (None, None, 0, 1))
    state = attend_stage(index, packed, state, far[:3], (None,) * 3)
    partial = attend_late(arrived.shape, index, packed, state, far[3:])

    returned = windowed(partial)
    here = jnp.where(mine, returned, 0).sum(0)
    after = moved(jnp.where(mine, 0, returned).sum(0), WINDOW)
    return merge_parts([here, after], local, local_lse).reshape(rows, draft, width)


def solution(mesh):
    placed = (
        P("group", None, "tensor"),
        P("group", None, None, "tensor"),
        P("group", None, None, "tensor"),
        P("group", "tensor", None, None, None),
        P(),
        P("group"),
        P("group"),
    )
    return jax.shard_map(
        on_device, mesh=mesh, in_specs=placed, out_specs=P("group", None, "tensor"), check_vma=False
    )
```

```python
import functools
import math

import jax
import jax.numpy as jnp
from jax import lax
from jax.experimental import pallas as pl
from jax.experimental.pallas import tpu as pltpu
from jax.sharding import PartitionSpec as P

WINDOW = 8
DRAFT = 2
BLOCK_ROWS = 16
FLIPS = ((0,), (1,), (2, 3), (4,), (5,), (6,), (7,))
STAGE_FLOPS = 10_000_000_000
LOCAL_FLOPS = 20_000_000_000
VMEM_BYTES = 16 * 1024 * 1024


def nt_dot(left, right):
    return lax.dot_general(left, right, (((1,), (1,)), ((), ())), preferred_element_type=jnp.float32)


def local_kernel(len_ref, q_ref, kv_ref, out_ref, lse_ref, scores):
    rows, vectors, head_dim = q_ref.shape
    slots = kv_ref.shape[2]
    cached = slots - 16
    scaling = head_dim ** (-0.5)
    place = lax.broadcasted_iota(jnp.int32, (vectors, slots), 1)
    token = lax.broadcasted_iota(jnp.int32, (vectors, slots), 0) // (vectors // DRAFT)
    fresh = (place >= cached) & (place - cached <= token)
    for row in range(rows):
        live = (place < jnp.minimum(len_ref[row], cached)) | fresh
        scores[row] = jnp.where(live, nt_dot(q_ref[row], kv_ref[row, 0]) * scaling, -jnp.inf)
    maxima = scores[...].max(-1, keepdims=True)
    weights = jnp.exp(scores[...] - maxima)
    totals = weights.sum(-1, keepdims=True)
    lse_ref[...] = jnp.broadcast_to(maxima + jnp.log(totals), lse_ref.shape)
    inverse = 1.0 / totals
    rounded = weights.astype(jnp.bfloat16)
    for row in range(rows):
        summed = jnp.dot(rounded[row], kv_ref[row, 1], preferred_element_type=jnp.float32)
        out_ref[row] = summed * inverse[row]


def local_attention(queries, own_kv, new_kv, own_len):
    rows, vectors, head_dim = queries.shape
    cache = jnp.concatenate([own_kv, new_kv], axis=1)
    cache = jnp.pad(cache, ((0, 0), (0, 16 - DRAFT), (0, 0), (0, 0)))
    cache = cache.transpose(0, 2, 1, 3)
    shape = jax.ShapeDtypeStruct((rows, vectors, head_dim), jnp.float32)
    vmem = pl.BlockSpec(memory_space=pltpu.VMEM)
    return pl.pallas_call(
        local_kernel,
        out_shape=(shape, shape),
        in_specs=[pl.BlockSpec(memory_space=pltpu.SMEM), vmem, vmem],
        out_specs=(vmem, vmem),
        scratch_shapes=[pltpu.VMEM((rows, vectors, cache.shape[2]), jnp.float32)],
        compiler_params=pltpu.CompilerParams(vmem_limit_bytes=VMEM_BYTES),
        cost_estimate=pl.CostEstimate(flops=LOCAL_FLOPS, bytes_accessed=2_500_000, transcendentals=70_000),
        name="local_attention",
    )(own_len, queries, cache)


def attend_block(q, kv_refs, scores):
    width, head_dim = q.shape
    scaling = head_dim ** (-0.5)
    maxima = None
    for part, kv in enumerate(kv_refs):
        product = nt_dot(q, kv[0])
        scores[part] = product
        top = product.max(-1, keepdims=True)
        maxima = top if maxima is None else jnp.maximum(maxima, top)
    base2 = scaling * math.log2(math.e)
    shift = maxima * base2
    totals = jnp.zeros((width, 1), jnp.float32)
    summed = jnp.zeros((width, head_dim), jnp.float32)
    for part, kv in enumerate(kv_refs):
        weights = jnp.exp2(scores[part] * base2 - shift)
        totals = totals + weights.sum(-1, keepdims=True)
        summed = summed + jnp.dot(weights.astype(jnp.bfloat16), kv[1], preferred_element_type=jnp.float32)
    level = jnp.broadcast_to(maxima * scaling + jnp.log(totals), (width, head_dim))
    return summed / totals, level


def pack_kernel(live_ref, q_ref, packed, index):
    cells, tiles, vectors, head_dim = q_ref.shape
    rows = tiles - 1
    packed[...] = jnp.zeros_like(packed)
    count = jnp.int32(0)
    for slot in range(cells * rows):
        packed[count] = q_ref[slot // rows, slot % rows]
        index[count] = slot
        count = count + live_ref[slot]
    index[cells * rows + 1] = count


def pack_queries(live, arrived):
    cells, tiles, vectors, head_dim = arrived.shape
    slots = cells * (tiles - 1)
    vmem, smem = pl.BlockSpec(memory_space=pltpu.VMEM), pl.BlockSpec(memory_space=pltpu.SMEM)
    return pl.pallas_call(
        pack_kernel,
        out_shape=(
            jax.ShapeDtypeStruct((slots + BLOCK_ROWS, vectors, head_dim), jnp.bfloat16),
            jax.ShapeDtypeStruct((slots + 2,), jnp.int32),
        ),
        in_specs=[smem, vmem],
        out_specs=(vmem, smem),
        compiler_params=pltpu.CompilerParams(vmem_limit_bytes=VMEM_BYTES),
        name="pack_queries",
    )(live, arrived)


def merged(first, second):
    top = jnp.maximum(first[1], second[1])
    first_scale, second_scale = jnp.exp(first[1] - top), jnp.exp(second[1] - top)
    totals = first_scale + second_scale
    return (first[0] * first_scale + second[0] * second_scale) / totals, top + jnp.log(totals)


def stage_kernel(parts, halves, index, packed, *rest):
    state, kv_refs, outs, scores = rest[: 2 * parts], rest[2 * parts : -3], rest[-3:-1], rest[-1]
    kv_refs = [kv if half is None else kv.at[half] for kv, half in zip(kv_refs, halves)]
    width, head_dim = outs[0].shape[1:]
    count = index[index.shape[0] - 1]

    def block(step, carry):
        q = packed[pl.ds(step * BLOCK_ROWS, BLOCK_ROWS)].reshape(width, head_dim)
        total = attend_block(q, kv_refs, scores)
        if parts:
            total = merged(total, (state[0][step], state[1][step]))
        outs[0][step], outs[1][step] = total
        return carry

    lax.fori_loop(0, (count + BLOCK_ROWS - 1) // BLOCK_ROWS, block, 0)


def attend_stage(index, packed, state, blocks, halves=(None, None)):
    slots, vectors, head_dim = packed.shape[0] - BLOCK_ROWS, *packed.shape[1:]
    chunk = blocks[0].shape[-2]
    width = BLOCK_ROWS * vectors
    vmem, smem = pl.BlockSpec(memory_space=pltpu.VMEM), pl.BlockSpec(memory_space=pltpu.SMEM)
    shape = jax.ShapeDtypeStruct((slots // BLOCK_ROWS, width, head_dim), jnp.float32)
    return pl.pallas_call(
        functools.partial(stage_kernel, len(state) // 2, halves),
        out_shape=(shape, shape),
        in_specs=[smem] + [vmem] * (1 + len(state) + len(blocks)),
        out_specs=(vmem, vmem),
        scratch_shapes=[pltpu.VMEM((len(blocks), width, chunk), jnp.float32)],
        compiler_params=pltpu.CompilerParams(vmem_limit_bytes=VMEM_BYTES),
        cost_estimate=pl.CostEstimate(flops=STAGE_FLOPS, bytes_accessed=2_000_000, transcendentals=0),
        name="attend_stage",
    )(index, packed, *state, *blocks)


def late_kernel(index, packed, attended_ref, level_ref, *rest):
    *kv_refs, out_ref, scores, stats = rest
    cells, tiles, vectors, head_dim = out_ref.shape
    rows = tiles - 1
    width = BLOCK_ROWS * vectors
    out_ref[...] = jnp.zeros_like(out_ref)
    stats[...] = jnp.zeros_like(stats)
    count = index[cells * rows + 1]

    lane = lax.broadcasted_iota(jnp.int32, (vectors, head_dim), 1)
    vector = lax.broadcasted_iota(jnp.int32, (vectors, head_dim), 0)
    on_lane = (lane % vectors == vector) & (lane < 3 * vectors)
    piece = lane // vectors

    def block(step, carry):
        first = step * BLOCK_ROWS
        q = packed[pl.ds(first, BLOCK_ROWS)].reshape(width, head_dim)
        late = attend_block(q, kv_refs, scores)
        attended, level = merged(late, (attended_ref[step], level_ref[step]))
        attended = attended.astype(jnp.bfloat16)
        high = level.astype(jnp.bfloat16).astype(jnp.float32)
        middle = (level - high).astype(jnp.bfloat16).astype(jnp.float32)
        low = level - high - middle
        for row in reversed(range(BLOCK_ROWS)):
            span = slice(row * vectors, (row + 1) * vectors)
            pieces = jnp.where(piece == 0, high[span], jnp.where(piece == 1, middle[span], low[span]))
            slot = index[first + jnp.where(first + row < count, row, 0)]
            out_ref[slot // rows, slot % rows] = attended[span]
            stats[pl.ds(slot, 1), :] = jnp.where(on_lane, pieces, 0.0).sum(0, keepdims=True)
        return carry

    lax.fori_loop(0, (count + BLOCK_ROWS - 1) // BLOCK_ROWS, block, 0)
    for cell in range(cells):
        out_ref[cell, rows] = stats[cell * rows : (cell + 1) * rows, :].astype(jnp.bfloat16)


def attend_late(shape, index, packed, state, blocks):
    cells, tiles, vectors, head_dim = shape
    slots = cells * (tiles - 1)
    chunk = blocks[0].shape[-2]
    width = BLOCK_ROWS * vectors
    vmem, smem = pl.BlockSpec(memory_space=pltpu.VMEM), pl.BlockSpec(memory_space=pltpu.SMEM)
    return pl.pallas_call(
        late_kernel,
        out_shape=jax.ShapeDtypeStruct(shape, jnp.bfloat16),
        in_specs=[smem] + [vmem] * (3 + len(blocks)),
        out_specs=vmem,
        scratch_shapes=[
            pltpu.VMEM((len(blocks), width, chunk), jnp.float32),
            pltpu.VMEM((slots, head_dim), jnp.float32),
        ],
        compiler_params=pltpu.CompilerParams(vmem_limit_bytes=VMEM_BYTES),
        cost_estimate=pl.CostEstimate(flops=STAGE_FLOPS, bytes_accessed=4_000_000, transcendentals=0),
        name="attend_late",
    )(index, packed, *state, *blocks)


def merge_kernel(*refs):
    *part_refs, local_ref, local_lse_ref, out_ref = refs
    rows, vectors, head_dim = local_ref.shape
    lane = lax.broadcasted_iota(jnp.int32, (vectors, head_dim), 1)
    vector = lax.broadcasted_iota(jnp.int32, (vectors, head_dim), 0)
    on_lane = (lane % vectors == vector) & (lane < 3 * vectors)
    pairs = [part_refs[k : k + 2] for k in range(0, len(part_refs), 2)]
    levels = [one[rows].astype(jnp.float32) + other[rows].astype(jnp.float32) for one, other in pairs]
    for row in range(rows):
        terms = [(local_ref[row], local_lse_ref[row])]
        for (one, other), level in zip(pairs, levels):
            line = jnp.broadcast_to(level[row : row + 1], (vectors, head_dim))
            lse = jnp.where(on_lane, line, 0.0).sum(-1, keepdims=True)
            attended = one[row].astype(jnp.float32) + other[row].astype(jnp.float32)
            terms.append((attended, jnp.broadcast_to(lse, (vectors, head_dim))))
        maxima = functools.reduce(jnp.maximum, [lse for _, lse in terms])
        scales = [jnp.exp(lse - maxima) for _, lse in terms]
        summed = sum(scale * term for scale, (term, _) in zip(scales, terms))
        out_ref[row] = (summed / sum(scales)).astype(jnp.bfloat16)


def merge_parts(parts, local, local_lse):
    vmem = pl.BlockSpec(memory_space=pltpu.VMEM)
    return pl.pallas_call(
        merge_kernel,
        out_shape=jax.ShapeDtypeStruct(local.shape, jnp.bfloat16),
        in_specs=[vmem] * (len(parts) + 2),
        out_specs=vmem,
        compiler_params=pltpu.CompilerParams(vmem_limit_bytes=VMEM_BYTES),
        name="merge_parts",
    )(*parts, local, local_lse)


def split_kernel(lane_ref, prefix_ref, *rest):
    *out_refs, by_head = rest
    sides = prefix_ref.shape[1]
    for side in range(sides):
        by_head[side] = jnp.swapaxes(prefix_ref[:, side], 0, 1)
    for out_ref, flips in zip(out_refs, FLIPS):
        for half, flip in enumerate(flips):
            for side in range(sides):
                target = out_ref if len(flips) == 1 else out_ref.at[half]
                target[side] = by_head[side, lane_ref[0] ^ flip]


def split_prefix(lane, prefix):
    positions, sides, heads, head_dim = prefix.shape
    shape = (sides, positions, head_dim)
    vmem = pl.BlockSpec(memory_space=pltpu.VMEM)
    return pl.pallas_call(
        split_kernel,
        out_shape=[
            jax.ShapeDtypeStruct(shape if len(flips) == 1 else (len(flips), *shape), prefix.dtype)
            for flips in FLIPS
        ],
        in_specs=[pl.BlockSpec(memory_space=pltpu.SMEM), vmem],
        out_specs=[vmem] * len(FLIPS),
        scratch_shapes=[pltpu.VMEM((sides, heads, positions, head_dim), prefix.dtype)],
        compiler_params=pltpu.CompilerParams(vmem_limit_bytes=VMEM_BYTES),
        cost_estimate=pl.CostEstimate(flops=0, bytes_accessed=4 * 1024 * 1024, transcendentals=0),
        name="split_prefix",
    )(lane.reshape(1), prefix)


def moved(x, by, flip=0):
    groups, lanes = lax.axis_size("group"), lax.axis_size("tensor")
    pairs = [
        (g * lanes + t, (g + by) % groups * lanes + (t ^ flip)) for g in range(groups) for t in range(lanes)
    ]
    return lax.ppermute(x, ("group", "tensor"), pairs)


def windowed(x):
    groups = lax.axis_size("group")
    windows = [list(range(first, first + WINDOW)) for first in range(0, groups, WINDOW)]
    return lax.all_to_all(x, "group", 0, 0, axis_index_groups=windows, tiled=True)


def on_device(queries, new_kv, own_kv, prefix_kv, owner, parent, own_len):
    rows, draft, width = queries.shape
    heads, head_dim = prefix_kv.shape[3:]
    per_kv = width // head_dim
    vectors = draft * per_kv
    me = lax.axis_index("group")
    place = me % WINDOW
    cells = jnp.arange(WINDOW)

    q = queries.reshape(rows, vectors, head_dim)
    distance = (me - owner[parent]) % lax.axis_size("group")
    tag = jnp.broadcast_to(distance.astype(jnp.bfloat16)[None, :, None], (1, rows, head_dim))
    sent = jnp.concatenate([q, tag.reshape(1, vectors, head_dim)])
    own, beside, near, *far = split_prefix(lax.axis_index("tensor"), prefix_kv[0])
    beside, far[2], sent = lax.optimization_barrier((moved(beside, 0, 1), far[2], sent))
    far[:3] = [moved(block, 0, 4 + step) for step, block in enumerate(far[:3])]
    near, after = moved(near, 0, 2), moved(sent, -WINDOW)

    mine = (cells < place)[:, None, None, None]
    cell = jnp.where(mine, sent, after)
    arrived = windowed(cell)
    tags = arrived[:, rows, :, 0].astype(jnp.int32)
    live = (tags > 0) & (tags == ((cells - place) % WINDOW)[:, None])
    own_kv, new_kv, far[3], cell = lax.optimization_barrier((own_kv, new_kv, far[3], cell))
    far[3] = moved(far[3], 0, 7)
    late_q, far[0] = lax.optimization_barrier((q, far[0]))
    local, local_lse = local_attention(late_q, own_kv, new_kv, own_len)
    arrived, local, local_lse = lax.optimization_barrier((arrived, local, local_lse))
    packed, index = pack_queries(live.reshape(-1).astype(jnp.int32), arrived)
    near_beside = moved(near, 0, 1)
    state = attend_stage(index, packed, (), [own, beside, far[0]], (None,) * 3)
    state = attend_stage(index, packed, state, [near, near_beside, *far[1:3]], (0, 1, None, None))
    partial = attend_late(arrived.shape, index, packed, state, far[3:])

    returned = windowed(partial)
    here = jnp.where(mine, returned, 0).sum(0)
    after = moved(jnp.where(mine, 0, returned).sum(0), WINDOW)
    return merge_parts([here, after], local, local_lse).reshape(rows, draft, width)


def solution(mesh):
    placed = (
        P("group", None, "tensor"),
        P("group", None, None, "tensor"),
        P("group", None, None, "tensor"),
        P("group", "tensor", None, None, None),
        P(),
        P("group"),
        P("group"),
    )
    return jax.shard_map(
        on_device, mesh=mesh, in_specs=placed, out_specs=P("group", None, "tensor"), check_vma=False
    )
```

```python
import functools
import math

import jax
import jax.numpy as jnp
from jax import lax
from jax.experimental import pallas as pl
from jax.experimental.pallas import tpu as pltpu
from jax.sharding import PartitionSpec as P

WINDOW = 8
DRAFT = 2
BLOCK_ROWS = 16
FLIPS = ((0,), (1,), (2, 3), (6,), (7,), (4,), (5,))
STAGE_FLOPS = 10_000_000_000
LOCAL_FLOPS = 20_000_000_000
VMEM_BYTES = 16 * 1024 * 1024


def nt_dot(left, right):
    return lax.dot_general(left, right, (((1,), (1,)), ((), ())), preferred_element_type=jnp.float32)


def local_kernel(len_ref, q_ref, kv_ref, out_ref, lse_ref, scores):
    rows, vectors, head_dim = q_ref.shape
    slots = kv_ref.shape[2]
    cached = slots - 16
    scaling = head_dim ** (-0.5)
    place = lax.broadcasted_iota(jnp.int32, (vectors, slots), 1)
    token = lax.broadcasted_iota(jnp.int32, (vectors, slots), 0) // (vectors // DRAFT)
    fresh = (place >= cached) & (place - cached <= token)
    for row in range(rows):
        live = (place < jnp.minimum(len_ref[row], cached)) | fresh
        scores[row] = jnp.where(live, nt_dot(q_ref[row], kv_ref[row, 0]) * scaling, -jnp.inf)
    maxima = scores[...].max(-1, keepdims=True)
    weights = jnp.exp(scores[...] - maxima)
    totals = weights.sum(-1, keepdims=True)
    lse_ref[...] = jnp.broadcast_to(maxima + jnp.log(totals), lse_ref.shape)
    inverse = 1.0 / totals
    rounded = weights.astype(jnp.bfloat16)
    for row in range(rows):
        summed = jnp.dot(rounded[row], kv_ref[row, 1], preferred_element_type=jnp.float32)
        out_ref[row] = summed * inverse[row]


def local_attention(queries, own_kv, new_kv, own_len):
    rows, vectors, head_dim = queries.shape
    cache = jnp.concatenate([own_kv, new_kv], axis=1)
    cache = jnp.pad(cache, ((0, 0), (0, 16 - DRAFT), (0, 0), (0, 0)))
    cache = cache.transpose(0, 2, 1, 3)
    shape = jax.ShapeDtypeStruct((rows, vectors, head_dim), jnp.float32)
    vmem = pl.BlockSpec(memory_space=pltpu.VMEM)
    return pl.pallas_call(
        local_kernel,
        out_shape=(shape, shape),
        in_specs=[pl.BlockSpec(memory_space=pltpu.SMEM), vmem, vmem],
        out_specs=(vmem, vmem),
        scratch_shapes=[pltpu.VMEM((rows, vectors, cache.shape[2]), jnp.float32)],
        compiler_params=pltpu.CompilerParams(vmem_limit_bytes=VMEM_BYTES),
        cost_estimate=pl.CostEstimate(flops=LOCAL_FLOPS, bytes_accessed=2_500_000, transcendentals=70_000),
        name="local_attention",
    )(own_len, queries, cache)


def attend_block(q, kv_refs, scores):
    width, head_dim = q.shape
    scaling = head_dim ** (-0.5)
    maxima = None
    for part, kv in enumerate(kv_refs):
        product = nt_dot(q, kv[0])
        scores[part] = product
        top = product.max(-1, keepdims=True)
        maxima = top if maxima is None else jnp.maximum(maxima, top)
    base2 = scaling * math.log2(math.e)
    shift = maxima * base2
    totals = jnp.zeros((width, 1), jnp.float32)
    summed = jnp.zeros((width, head_dim), jnp.float32)
    for part, kv in enumerate(kv_refs):
        weights = jnp.exp2(scores[part] * base2 - shift)
        totals = totals + weights.sum(-1, keepdims=True)
        summed = summed + jnp.dot(weights.astype(jnp.bfloat16), kv[1], preferred_element_type=jnp.float32)
    level = jnp.broadcast_to(maxima * scaling + jnp.log(totals), (width, head_dim))
    return summed / totals, level


def pack_kernel(live_ref, q_ref, packed, index):
    cells, tiles, vectors, head_dim = q_ref.shape
    rows = tiles - 1
    packed[...] = jnp.zeros_like(packed)
    count = jnp.int32(0)
    for slot in range(cells * rows):
        packed[count] = q_ref[slot // rows, slot % rows]
        index[count] = slot
        count = count + live_ref[slot]
    index[cells * rows + 1] = count


def pack_queries(live, arrived):
    cells, tiles, vectors, head_dim = arrived.shape
    slots = cells * (tiles - 1)
    vmem, smem = pl.BlockSpec(memory_space=pltpu.VMEM), pl.BlockSpec(memory_space=pltpu.SMEM)
    return pl.pallas_call(
        pack_kernel,
        out_shape=(
            jax.ShapeDtypeStruct((slots + BLOCK_ROWS, vectors, head_dim), jnp.bfloat16),
            jax.ShapeDtypeStruct((slots + 2,), jnp.int32),
        ),
        in_specs=[smem, vmem],
        out_specs=(vmem, smem),
        compiler_params=pltpu.CompilerParams(vmem_limit_bytes=VMEM_BYTES),
        name="pack_queries",
    )(live, arrived)


def merged(first, second):
    top = jnp.maximum(first[1], second[1])
    first_scale, second_scale = jnp.exp(first[1] - top), jnp.exp(second[1] - top)
    totals = first_scale + second_scale
    return (first[0] * first_scale + second[0] * second_scale) / totals, top + jnp.log(totals)


def stage_kernel(parts, halves, index, packed, *rest):
    state, kv_refs, outs, scores = rest[: 2 * parts], rest[2 * parts : -3], rest[-3:-1], rest[-1]
    kv_refs = [kv if half is None else kv.at[half] for kv, half in zip(kv_refs, halves)]
    width, head_dim = outs[0].shape[1:]
    count = index[index.shape[0] - 1]

    def block(step, carry):
        q = packed[pl.ds(step * BLOCK_ROWS, BLOCK_ROWS)].reshape(width, head_dim)
        total = attend_block(q, kv_refs, scores)
        if parts:
            total = merged(total, (state[0][step], state[1][step]))
        outs[0][step], outs[1][step] = total
        return carry

    lax.fori_loop(0, (count + BLOCK_ROWS - 1) // BLOCK_ROWS, block, 0)


def attend_stage(index, packed, state, blocks, halves=(None, None)):
    slots, vectors, head_dim = packed.shape[0] - BLOCK_ROWS, *packed.shape[1:]
    chunk = blocks[0].shape[-2]
    width = BLOCK_ROWS * vectors
    vmem, smem = pl.BlockSpec(memory_space=pltpu.VMEM), pl.BlockSpec(memory_space=pltpu.SMEM)
    shape = jax.ShapeDtypeStruct((slots // BLOCK_ROWS, width, head_dim), jnp.float32)
    return pl.pallas_call(
        functools.partial(stage_kernel, len(state) // 2, halves),
        out_shape=(shape, shape),
        in_specs=[smem] + [vmem] * (1 + len(state) + len(blocks)),
        out_specs=(vmem, vmem),
        scratch_shapes=[pltpu.VMEM((len(blocks), width, chunk), jnp.float32)],
        compiler_params=pltpu.CompilerParams(vmem_limit_bytes=VMEM_BYTES),
        cost_estimate=pl.CostEstimate(flops=STAGE_FLOPS, bytes_accessed=2_000_000, transcendentals=0),
        name="attend_stage",
    )(index, packed, *state, *blocks)


def late_kernel(index, packed, attended_ref, level_ref, *rest):
    *kv_refs, out_ref, scores, stats = rest
    cells, tiles, vectors, head_dim = out_ref.shape
    rows = tiles - 1
    width = BLOCK_ROWS * vectors
    out_ref[...] = jnp.zeros_like(out_ref)
    stats[...] = jnp.zeros_like(stats)
    count = index[cells * rows + 1]

    lane = lax.broadcasted_iota(jnp.int32, (vectors, head_dim), 1)
    vector = lax.broadcasted_iota(jnp.int32, (vectors, head_dim), 0)
    on_lane = (lane % vectors == vector) & (lane < 3 * vectors)
    piece = lane // vectors

    def block(step, carry):
        first = step * BLOCK_ROWS
        q = packed[pl.ds(first, BLOCK_ROWS)].reshape(width, head_dim)
        late = attend_block(q, kv_refs, scores)
        attended, level = merged(late, (attended_ref[step], level_ref[step]))
        attended = attended.astype(jnp.bfloat16)
        high = level.astype(jnp.bfloat16).astype(jnp.float32)
        middle = (level - high).astype(jnp.bfloat16).astype(jnp.float32)
        low = level - high - middle
        for row in reversed(range(BLOCK_ROWS)):
            span = slice(row * vectors, (row + 1) * vectors)
            pieces = jnp.where(piece == 0, high[span], jnp.where(piece == 1, middle[span], low[span]))
            slot = index[first + jnp.where(first + row < count, row, 0)]
            out_ref[slot // rows, slot % rows] = attended[span]
            stats[pl.ds(slot, 1), :] = jnp.where(on_lane, pieces, 0.0).sum(0, keepdims=True)
        return carry

    lax.fori_loop(0, (count + BLOCK_ROWS - 1) // BLOCK_ROWS, block, 0)
    for cell in range(cells):
        out_ref[cell, rows] = stats[cell * rows : (cell + 1) * rows, :].astype(jnp.bfloat16)


def attend_late(shape, index, packed, state, blocks):
    cells, tiles, vectors, head_dim = shape
    slots = cells * (tiles - 1)
    chunk = blocks[0].shape[-2]
    width = BLOCK_ROWS * vectors
    vmem, smem = pl.BlockSpec(memory_space=pltpu.VMEM), pl.BlockSpec(memory_space=pltpu.SMEM)
    return pl.pallas_call(
        late_kernel,
        out_shape=jax.ShapeDtypeStruct(shape, jnp.bfloat16),
        in_specs=[smem] + [vmem] * (3 + len(blocks)),
        out_specs=vmem,
        scratch_shapes=[
            pltpu.VMEM((len(blocks), width, chunk), jnp.float32),
            pltpu.VMEM((slots, head_dim), jnp.float32),
        ],
        compiler_params=pltpu.CompilerParams(vmem_limit_bytes=VMEM_BYTES),
        cost_estimate=pl.CostEstimate(flops=STAGE_FLOPS, bytes_accessed=4_000_000, transcendentals=0),
        name="attend_late",
    )(index, packed, *state, *blocks)


def merge_kernel(*refs):
    *part_refs, local_ref, local_lse_ref, out_ref = refs
    rows, vectors, head_dim = local_ref.shape
    lane = lax.broadcasted_iota(jnp.int32, (vectors, head_dim), 1)
    vector = lax.broadcasted_iota(jnp.int32, (vectors, head_dim), 0)
    on_lane = (lane % vectors == vector) & (lane < 3 * vectors)
    pairs = [part_refs[k : k + 2] for k in range(0, len(part_refs), 2)]
    levels = [one[rows].astype(jnp.float32) + other[rows].astype(jnp.float32) for one, other in pairs]
    for row in range(rows):
        terms = [(local_ref[row], local_lse_ref[row])]
        for (one, other), level in zip(pairs, levels):
            line = jnp.broadcast_to(level[row : row + 1], (vectors, head_dim))
            lse = jnp.where(on_lane, line, 0.0).sum(-1, keepdims=True)
            attended = one[row].astype(jnp.float32) + other[row].astype(jnp.float32)
            terms.append((attended, jnp.broadcast_to(lse, (vectors, head_dim))))
        maxima = functools.reduce(jnp.maximum, [lse for _, lse in terms])
        scales = [jnp.exp(lse - maxima) for _, lse in terms]
        summed = sum(scale * term for scale, (term, _) in zip(scales, terms))
        out_ref[row] = (summed / sum(scales)).astype(jnp.bfloat16)


def merge_parts(parts, local, local_lse):
    vmem = pl.BlockSpec(memory_space=pltpu.VMEM)
    return pl.pallas_call(
        merge_kernel,
        out_shape=jax.ShapeDtypeStruct(local.shape, jnp.bfloat16),
        in_specs=[vmem] * (len(parts) + 2),
        out_specs=vmem,
        compiler_params=pltpu.CompilerParams(vmem_limit_bytes=VMEM_BYTES),
        name="merge_parts",
    )(*parts, local, local_lse)


def split_kernel(lane_ref, prefix_ref, *rest):
    *out_refs, by_head = rest
    sides = prefix_ref.shape[1]
    for side in range(sides):
        by_head[side] = jnp.swapaxes(prefix_ref[:, side], 0, 1)
    for out_ref, flips in zip(out_refs, FLIPS):
        for half, flip in enumerate(flips):
            for side in range(sides):
                target = out_ref if len(flips) == 1 else out_ref.at[half]
                target[side] = by_head[side, lane_ref[0] ^ flip]


def split_prefix(lane, prefix):
    positions, sides, heads, head_dim = prefix.shape
    shape = (sides, positions, head_dim)
    vmem = pl.BlockSpec(memory_space=pltpu.VMEM)
    return pl.pallas_call(
        split_kernel,
        out_shape=[
            jax.ShapeDtypeStruct(shape if len(flips) == 1 else (len(flips), *shape), prefix.dtype)
            for flips in FLIPS
        ],
        in_specs=[pl.BlockSpec(memory_space=pltpu.SMEM), vmem],
        out_specs=[vmem] * len(FLIPS),
        scratch_shapes=[pltpu.VMEM((sides, heads, positions, head_dim), prefix.dtype)],
        compiler_params=pltpu.CompilerParams(vmem_limit_bytes=VMEM_BYTES),
        cost_estimate=pl.CostEstimate(flops=0, bytes_accessed=4 * 1024 * 1024, transcendentals=0),
        name="split_prefix",
    )(lane.reshape(1), prefix)


def moved(x, by, flip=0):
    groups, lanes = lax.axis_size("group"), lax.axis_size("tensor")
    pairs = [
        (g * lanes + t, (g + by) % groups * lanes + (t ^ flip)) for g in range(groups) for t in range(lanes)
    ]
    return lax.ppermute(x, ("group", "tensor"), pairs)


def windowed(x):
    groups = lax.axis_size("group")
    windows = [list(range(first, first + WINDOW)) for first in range(0, groups, WINDOW)]
    return lax.all_to_all(x, "group", 0, 0, axis_index_groups=windows, tiled=True)


def on_device(queries, new_kv, own_kv, prefix_kv, owner, parent, own_len):
    rows, draft, width = queries.shape
    heads, head_dim = prefix_kv.shape[3:]
    per_kv = width // head_dim
    vectors = draft * per_kv
    me = lax.axis_index("group")
    place = me % WINDOW
    cells = jnp.arange(WINDOW)

    q = queries.reshape(rows, vectors, head_dim)
    distance = (me - owner[parent]) % lax.axis_size("group")
    tag = jnp.broadcast_to(distance.astype(jnp.bfloat16)[None, :, None], (1, rows, head_dim))
    sent = jnp.concatenate([q, tag.reshape(1, vectors, head_dim)])
    own, beside, near, *far = split_prefix(lax.axis_index("tensor"), prefix_kv[0])
    beside, far[2], sent = lax.optimization_barrier((moved(beside, 0, 1), far[2], sent))
    far[:3] = [moved(block, 0, flip) for flip, block in zip((6, 7, 4), far[:3])]
    near, after = moved(near, 0, 2), moved(sent, -WINDOW)

    mine = (cells < place)[:, None, None, None]
    cell = jnp.where(mine, sent, after)
    arrived = windowed(cell)
    tags = arrived[:, rows, :, 0].astype(jnp.int32)
    live = (tags > 0) & (tags == ((cells - place) % WINDOW)[:, None])
    own_kv, new_kv, far[3], cell = lax.optimization_barrier((own_kv, new_kv, far[3], cell))
    far[3] = moved(far[3], 0, 5)
    late_q, far[0] = lax.optimization_barrier((q, far[0]))
    local, local_lse = local_attention(late_q, own_kv, new_kv, own_len)
    arrived, local, local_lse = lax.optimization_barrier((arrived, local, local_lse))
    packed, index = pack_queries(live.reshape(-1).astype(jnp.int32), arrived)
    near_beside = moved(near, 0, 1)
    state = attend_stage(index, packed, (), [own, beside, far[0]], (None,) * 3)
    state = attend_stage(index, packed, state, [near, near_beside, *far[1:3]], (0, 1, None, None))
    partial = attend_late(arrived.shape, index, packed, state, far[3:])

    returned = windowed(partial)
    here = jnp.where(mine, returned, 0).sum(0)
    after = moved(jnp.where(mine, 0, returned).sum(0), WINDOW)
    return merge_parts([here, after], local, local_lse).reshape(rows, draft, width)


def solution(mesh):
    placed = (
        P("group", None, "tensor"),
        P("group", None, None, "tensor"),
        P("group", None, None, "tensor"),
        P("group", "tensor", None, None, None),
        P(),
        P("group"),
        P("group"),
    )
    return jax.shard_map(
        on_device, mesh=mesh, in_specs=placed, out_specs=P("group", None, "tensor"), check_vma=False
    )
```

```python
import functools
import math

import jax
import jax.numpy as jnp
from jax import lax
from jax.experimental import pallas as pl
from jax.experimental.pallas import tpu as pltpu
from jax.sharding import PartitionSpec as P

WINDOW = 8
DRAFT = 2
BLOCK_ROWS = 16
FLIPS = ((0,), (1,), (2, 3), (4,), (5,), (6,), (7,))
STAGE_FLOPS = 10_000_000_000
LOCAL_FLOPS = 20_000_000_000
VMEM_BYTES = 16 * 1024 * 1024


def nt_dot(left, right):
    return lax.dot_general(left, right, (((1,), (1,)), ((), ())), preferred_element_type=jnp.float32)


def local_kernel(len_ref, q_ref, kv_ref, out_ref, lse_ref, scores):
    rows, vectors, head_dim = q_ref.shape
    slots = kv_ref.shape[2]
    cached = slots - 16
    scaling = head_dim ** (-0.5)
    place = lax.broadcasted_iota(jnp.int32, (vectors, slots), 1)
    token = lax.broadcasted_iota(jnp.int32, (vectors, slots), 0) // (vectors // DRAFT)
    fresh = (place >= cached) & (place - cached <= token)
    for row in range(rows):
        live = (place < jnp.minimum(len_ref[row], cached)) | fresh
        scores[row] = jnp.where(live, nt_dot(q_ref[row], kv_ref[row, 0]) * scaling, -jnp.inf)
    maxima = scores[...].max(-1, keepdims=True)
    weights = jnp.exp(scores[...] - maxima)
    totals = weights.sum(-1, keepdims=True)
    lse_ref[...] = jnp.broadcast_to(maxima + jnp.log(totals), lse_ref.shape)
    inverse = 1.0 / totals
    rounded = weights.astype(jnp.bfloat16)
    for row in range(rows):
        summed = jnp.dot(rounded[row], kv_ref[row, 1], preferred_element_type=jnp.float32)
        out_ref[row] = summed * inverse[row]


def local_attention(queries, own_kv, new_kv, own_len):
    rows, vectors, head_dim = queries.shape
    cache = jnp.concatenate([own_kv, new_kv], axis=1)
    cache = jnp.pad(cache, ((0, 0), (0, 16 - DRAFT), (0, 0), (0, 0)))
    cache = cache.transpose(0, 2, 1, 3)
    shape = jax.ShapeDtypeStruct((rows, vectors, head_dim), jnp.float32)
    vmem = pl.BlockSpec(memory_space=pltpu.VMEM)
    return pl.pallas_call(
        local_kernel,
        out_shape=(shape, shape),
        in_specs=[pl.BlockSpec(memory_space=pltpu.SMEM), vmem, vmem],
        out_specs=(vmem, vmem),
        scratch_shapes=[pltpu.VMEM((rows, vectors, cache.shape[2]), jnp.float32)],
        compiler_params=pltpu.CompilerParams(vmem_limit_bytes=VMEM_BYTES),
        cost_estimate=pl.CostEstimate(flops=LOCAL_FLOPS, bytes_accessed=2_500_000, transcendentals=70_000),
        name="local_attention",
    )(own_len, queries, cache)


def attend_block(q, kv_refs, scores):
    width, head_dim = q.shape
    scaling = head_dim ** (-0.5)
    maxima = None
    for part, kv in enumerate(kv_refs):
        product = nt_dot(q, kv[0])
        scores[part] = product
        top = product.max(-1, keepdims=True)
        maxima = top if maxima is None else jnp.maximum(maxima, top)
    base2 = scaling * math.log2(math.e)
    shift = maxima * base2
    totals = jnp.zeros((width, 1), jnp.float32)
    summed = jnp.zeros((width, head_dim), jnp.float32)
    for part, kv in enumerate(kv_refs):
        weights = jnp.exp2(scores[part] * base2 - shift)
        totals = totals + weights.sum(-1, keepdims=True)
        summed = summed + jnp.dot(weights.astype(jnp.bfloat16), kv[1], preferred_element_type=jnp.float32)
    level = jnp.broadcast_to(maxima * scaling + jnp.log(totals), (width, head_dim))
    return summed / totals, level


def pack_kernel(live_ref, q_ref, packed, index):
    cells, tiles, vectors, head_dim = q_ref.shape
    rows = tiles - 1
    packed[...] = jnp.zeros_like(packed)
    count = jnp.int32(0)
    for slot in range(cells * rows):
        packed[count] = q_ref[slot // rows, slot % rows]
        index[count] = slot
        count = count + live_ref[slot]
    index[cells * rows + 1] = count


def pack_queries(live, arrived):
    cells, tiles, vectors, head_dim = arrived.shape
    slots = cells * (tiles - 1)
    vmem, smem = pl.BlockSpec(memory_space=pltpu.VMEM), pl.BlockSpec(memory_space=pltpu.SMEM)
    return pl.pallas_call(
        pack_kernel,
        out_shape=(
            jax.ShapeDtypeStruct((slots + BLOCK_ROWS, vectors, head_dim), jnp.bfloat16),
            jax.ShapeDtypeStruct((slots + 2,), jnp.int32),
        ),
        in_specs=[smem, vmem],
        out_specs=(vmem, smem),
        compiler_params=pltpu.CompilerParams(vmem_limit_bytes=VMEM_BYTES),
        name="pack_queries",
    )(live, arrived)


def merged(first, second):
    top = jnp.maximum(first[1], second[1])
    first_scale, second_scale = jnp.exp(first[1] - top), jnp.exp(second[1] - top)
    totals = first_scale + second_scale
    return (first[0] * first_scale + second[0] * second_scale) / totals, top + jnp.log(totals)


def stage_kernel(parts, halves, index, packed, *rest):
    state, kv_refs, outs, scores = rest[: 2 * parts], rest[2 * parts : -3], rest[-3:-1], rest[-1]
    kv_refs = [kv if half is None else kv.at[half] for kv, half in zip(kv_refs, halves)]
    width, head_dim = outs[0].shape[1:]
    count = index[index.shape[0] - 1]

    def block(step, carry):
        q = packed[pl.ds(step * BLOCK_ROWS, BLOCK_ROWS)].reshape(width, head_dim)
        total = attend_block(q, kv_refs, scores)
        if parts:
            total = merged(total, (state[0][step], state[1][step]))
        outs[0][step], outs[1][step] = total
        return carry

    lax.fori_loop(0, (count + BLOCK_ROWS - 1) // BLOCK_ROWS, block, 0)


def attend_stage(index, packed, state, blocks, halves=(None, None)):
    slots, vectors, head_dim = packed.shape[0] - BLOCK_ROWS, *packed.shape[1:]
    chunk = blocks[0].shape[-2]
    width = BLOCK_ROWS * vectors
    vmem, smem = pl.BlockSpec(memory_space=pltpu.VMEM), pl.BlockSpec(memory_space=pltpu.SMEM)
    shape = jax.ShapeDtypeStruct((slots // BLOCK_ROWS, width, head_dim), jnp.float32)
    return pl.pallas_call(
        functools.partial(stage_kernel, len(state) // 2, halves),
        out_shape=(shape, shape),
        in_specs=[smem] + [vmem] * (1 + len(state) + len(blocks)),
        out_specs=(vmem, vmem),
        scratch_shapes=[pltpu.VMEM((len(blocks), width, chunk), jnp.float32)],
        compiler_params=pltpu.CompilerParams(vmem_limit_bytes=VMEM_BYTES),
        cost_estimate=pl.CostEstimate(flops=STAGE_FLOPS, bytes_accessed=2_000_000, transcendentals=0),
        name="attend_stage",
    )(index, packed, *state, *blocks)


def late_kernel(index, packed, attended_ref, level_ref, *rest):
    *kv_refs, out_ref, scores, stats = rest
    cells, tiles, vectors, head_dim = out_ref.shape
    rows = tiles - 1
    width = BLOCK_ROWS * vectors
    out_ref[...] = jnp.zeros_like(out_ref)
    stats[...] = jnp.zeros_like(stats)
    count = index[cells * rows + 1]

    lane = lax.broadcasted_iota(jnp.int32, (vectors, head_dim), 1)
    vector = lax.broadcasted_iota(jnp.int32, (vectors, head_dim), 0)
    on_lane = (lane % vectors == vector) & (lane < 3 * vectors)
    piece = lane // vectors

    def block(step, carry):
        first = step * BLOCK_ROWS
        q = packed[pl.ds(first, BLOCK_ROWS)].reshape(width, head_dim)
        late = attend_block(q, kv_refs, scores)
        attended, level = merged(late, (attended_ref[step], level_ref[step]))
        attended = attended.astype(jnp.bfloat16)
        high = level.astype(jnp.bfloat16).astype(jnp.float32)
        middle = (level - high).astype(jnp.bfloat16).astype(jnp.float32)
        low = level - high - middle
        for row in reversed(range(BLOCK_ROWS)):
            span = slice(row * vectors, (row + 1) * vectors)
            pieces = jnp.where(piece == 0, high[span], jnp.where(piece == 1, middle[span], low[span]))
            slot = index[first + jnp.where(first + row < count, row, 0)]
            out_ref[slot // rows, slot % rows] = attended[span]
            stats[pl.ds(slot, 1), :] = jnp.where(on_lane, pieces, 0.0).sum(0, keepdims=True)
        return carry

    lax.fori_loop(0, (count + BLOCK_ROWS - 1) // BLOCK_ROWS, block, 0)
    for cell in range(cells):
        out_ref[cell, rows] = stats[cell * rows : (cell + 1) * rows, :].astype(jnp.bfloat16)


def attend_late(shape, index, packed, state, blocks):
    cells, tiles, vectors, head_dim = shape
    slots = cells * (tiles - 1)
    chunk = blocks[0].shape[-2]
    width = BLOCK_ROWS * vectors
    vmem, smem = pl.BlockSpec(memory_space=pltpu.VMEM), pl.BlockSpec(memory_space=pltpu.SMEM)
    return pl.pallas_call(
        late_kernel,
        out_shape=jax.ShapeDtypeStruct(shape, jnp.bfloat16),
        in_specs=[smem] + [vmem] * (3 + len(blocks)),
        out_specs=vmem,
        scratch_shapes=[
            pltpu.VMEM((len(blocks), width, chunk), jnp.float32),
            pltpu.VMEM((slots, head_dim), jnp.float32),
        ],
        compiler_params=pltpu.CompilerParams(vmem_limit_bytes=VMEM_BYTES),
        cost_estimate=pl.CostEstimate(flops=STAGE_FLOPS, bytes_accessed=4_000_000, transcendentals=0),
        name="attend_late",
    )(index, packed, *state, *blocks)


def merge_kernel(*refs):
    *part_refs, local_ref, local_lse_ref, out_ref = refs
    rows, vectors, head_dim = local_ref.shape
    lane = lax.broadcasted_iota(jnp.int32, (vectors, head_dim), 1)
    vector = lax.broadcasted_iota(jnp.int32, (vectors, head_dim), 0)
    on_lane = (lane % vectors == vector) & (lane < 3 * vectors)
    pairs = [part_refs[k : k + 2] for k in range(0, len(part_refs), 2)]
    levels = [one[rows].astype(jnp.float32) + other[rows].astype(jnp.float32) for one, other in pairs]
    for row in range(rows):
        terms = [(local_ref[row], local_lse_ref[row])]
        for (one, other), level in zip(pairs, levels):
            line = jnp.broadcast_to(level[row : row + 1], (vectors, head_dim))
            lse = jnp.where(on_lane, line, 0.0).sum(-1, keepdims=True)
            attended = one[row].astype(jnp.float32) + other[row].astype(jnp.float32)
            terms.append((attended, jnp.broadcast_to(lse, (vectors, head_dim))))
        maxima = functools.reduce(jnp.maximum, [lse for _, lse in terms])
        scales = [jnp.exp(lse - maxima) for _, lse in terms]
        summed = sum(scale * term for scale, (term, _) in zip(scales, terms))
        out_ref[row] = (summed / sum(scales)).astype(jnp.bfloat16)


def merge_parts(parts, local, local_lse):
    vmem = pl.BlockSpec(memory_space=pltpu.VMEM)
    return pl.pallas_call(
        merge_kernel,
        out_shape=jax.ShapeDtypeStruct(local.shape, jnp.bfloat16),
        in_specs=[vmem] * (len(parts) + 2),
        out_specs=vmem,
        compiler_params=pltpu.CompilerParams(vmem_limit_bytes=VMEM_BYTES),
        name="merge_parts",
    )(*parts, local, local_lse)


def split_kernel(lane_ref, prefix_ref, *rest):
    *out_refs, by_head = rest
    sides = prefix_ref.shape[1]
    for side in range(sides):
        by_head[side] = jnp.swapaxes(prefix_ref[:, side], 0, 1)
    for out_ref, flips in zip(out_refs, FLIPS):
        for half, flip in enumerate(flips):
            for side in range(sides):
                target = out_ref if len(flips) == 1 else out_ref.at[half]
                target[side] = by_head[side, lane_ref[0] ^ flip]


def split_prefix(lane, prefix):
    positions, sides, heads, head_dim = prefix.shape
    shape = (sides, positions, head_dim)
    vmem = pl.BlockSpec(memory_space=pltpu.VMEM)
    return pl.pallas_call(
        split_kernel,
        out_shape=[
            jax.ShapeDtypeStruct(shape if len(flips) == 1 else (len(flips), *shape), prefix.dtype)
            for flips in FLIPS
        ],
        in_specs=[pl.BlockSpec(memory_space=pltpu.SMEM), vmem],
        out_specs=[vmem] * len(FLIPS),
        scratch_shapes=[pltpu.VMEM((sides, heads, positions, head_dim), prefix.dtype)],
        compiler_params=pltpu.CompilerParams(vmem_limit_bytes=VMEM_BYTES),
        cost_estimate=pl.CostEstimate(flops=0, bytes_accessed=4 * 1024 * 1024, transcendentals=0),
        name="split_prefix",
    )(lane.reshape(1), prefix)


def moved(x, by, flip=0):
    groups, lanes = lax.axis_size("group"), lax.axis_size("tensor")
    pairs = [
        (g * lanes + t, (g + by) % groups * lanes + (t ^ flip)) for g in range(groups) for t in range(lanes)
    ]
    return lax.ppermute(x, ("group", "tensor"), pairs)


def windowed(x):
    groups = lax.axis_size("group")
    windows = [list(range(first, first + WINDOW)) for first in range(0, groups, WINDOW)]
    return lax.all_to_all(x, "group", 0, 0, axis_index_groups=windows, tiled=True)


def on_device(queries, new_kv, own_kv, prefix_kv, owner, parent, own_len):
    rows, draft, width = queries.shape
    heads, head_dim = prefix_kv.shape[3:]
    per_kv = width // head_dim
    vectors = draft * per_kv
    me = lax.axis_index("group")
    place = me % WINDOW
    cells = jnp.arange(WINDOW)

    q = queries.reshape(rows, vectors, head_dim)
    distance = (me - owner[parent]) % lax.axis_size("group")
    tag = jnp.broadcast_to(distance.astype(jnp.bfloat16)[None, :, None], (1, rows, head_dim))
    sent = jnp.concatenate([q, tag.reshape(1, vectors, head_dim)])
    own, beside, near, *far = split_prefix(lax.axis_index("tensor"), prefix_kv[0])
    beside, far[2], sent = lax.optimization_barrier((moved(beside, 0, 1), far[2], sent))
    far[:3] = [moved(block, 0, 4 + step) for step, block in enumerate(far[:3])]
    near, after = moved(near, 0, 2), moved(sent, -WINDOW)

    mine = (cells < place)[:, None, None, None]
    cell = jnp.where(mine, sent, after)
    arrived = windowed(cell)
    tags = arrived[:, rows, :, 0].astype(jnp.int32)
    live = (tags > 0) & (tags == ((cells - place) % WINDOW)[:, None])
    own_kv, new_kv, far[3], cell = lax.optimization_barrier((own_kv, new_kv, far[3], cell))
    far[3] = moved(far[3], 0, 7)
    late_q, far[0] = lax.optimization_barrier((q, far[0]))
    local, local_lse = local_attention(late_q, own_kv, new_kv, own_len)
    arrived, local, local_lse = lax.optimization_barrier((arrived, local, local_lse))
    packed, index = pack_queries(live.reshape(-1).astype(jnp.int32), arrived)
    near_beside = moved(near, 0, 1)
    state = attend_stage(index, packed, (), [own, beside, *far[:2]], (None,) * 4)
    state = attend_stage(index, packed, state, [near, near_beside, far[2]], (0, 1, None))
    partial = attend_late(arrived.shape, index, packed, state, far[3:])

    returned = windowed(partial)
    here = jnp.where(mine, returned, 0).sum(0)
    after = moved(jnp.where(mine, 0, returned).sum(0), WINDOW)
    return merge_parts([here, after], local, local_lse).reshape(rows, draft, width)


def solution(mesh):
    placed = (
        P("group", None, "tensor"),
        P("group", None, None, "tensor"),
        P("group", None, None, "tensor"),
        P("group", "tensor", None, None, None),
        P(),
        P("group"),
        P("group"),
    )
    return jax.shard_map(
        on_device, mesh=mesh, in_specs=placed, out_specs=P("group", None, "tensor"), check_vma=False
    )
```
